512 devices in a mesh: dp: 64 (over y, z), mp: 8 (over x, core).
Axes of the slice: x: 4, y: 4, z: 16, core: 2. Of those that a mesh axis runs over, the one named last changes fastest.
Arguments:
- grads: bfloat16 [64, 64, 512, 256], P('dp', None, 'mp'), may hold values from -16 to 16
- momentum: float32 [64, 512, 256], P('dp', 'mp'), may hold values from -24 to 24
- slots: int32 [64], replicated, may hold values from 0 to 63, each once
Outputs:
- updates: bfloat16 [64, 512, 256], P(None, 'mp')
- new_momentum: float32 [64, 512, 256], P('dp', 'mp')
The draws below stay inside these ranges and needn't reach their ends.
Inputs may be any that keep to these rules, and one draw needn't show every extreme that they name: slots is a permutation; matrix i is owned by index slots[i] of dp.
All inputs are finite; a program needn't handle non-finite values.
Results may differ from the reference program's by a relative error of at most 0.001.
Values may be sent and summed in bfloat16 or wider, within the bound.
A program may use at most 64 MiB of HBM per device.

```python
import math
import jax
import jax.numpy as jnp
from jax import lax

KVR = 512
HD = 256
MATS = 64
ITERS = 5
N_DP = 64


def strengthened(values, rng, source, target, shards_of, factor):
    owner, partner = [(jnp.arange(values.shape[position]) // (values.shape[position] // shards_of)).reshape([-1 if axis == position else 1 for axis in range(values.ndim)]) for position in (source, target)]
    chosen = jax.random.permutation(rng, shards_of)[partner]
    strong = (owner == chosen) | (owner == (partner + shards_of // 2) % shards_of)
    return jnp.where(strong, factor * values, values)


def shard_levels(rng, dims, shards, least, high):
    gain, own = 1.0, jax.random.fold_in(rng, 6)
    for position, blocks in shards:
        heights = jnp.exp(jax.random.uniform(jax.random.fold_in(own, position), (blocks,), jnp.float32, least / len(shards), high / len(shards)))
        gain = gain * jnp.repeat(heights, dims[position] // blocks).reshape([-1 if axis == position else 1 for axis in range(len(dims))])
    return gain


def normal_values(rng, dims, deviation, bound, cuts=(), dtype=jnp.bfloat16):
    result = jax.random.normal(rng, dims, jnp.float32) * deviation
    if len(cuts) > 0:
        result = shard_levels(rng, dims, cuts, -0.22, 0.18) * result
    return jnp.clip(result, min=-bound, max=bound).astype(dtype)


def heavy_noise(own_key, shape, scale, reach, cuts, heavy, held_as=jnp.bfloat16):
    result = scale * jax.random.normal(own_key, shape, jnp.float32)
    if cuts:
        result = result * shard_levels(own_key, shape, cuts, -0.22, 0.18)
    return jnp.clip(strengthened(result, jax.random.fold_in(own_key, 3), *heavy), -reach, reach).astype(held_as)


def setup_inputs(seed: int = 0) -> dict:
    arg_keys = jax.random.split(jax.random.key(seed), 4)
    return {
        "grads": heavy_noise(arg_keys[0], (N_DP, MATS, KVR, HD), 1.0, 16.0, ((0, 64), (2, 8)), (0, 1, 64, 4.0)),
        "momentum": normal_values(arg_keys[1], (MATS, KVR, HD), 4.0, 24.0, ((0, 64), (1, 8)), jnp.float32),
        "slots": jax.random.permutation(arg_keys[2], MATS).astype(jnp.int32),
    }


coef_a = 3.4445
coef_b = -4.775
coef_c = 2.0315

def orthogonalize(blended):
    iterate = blended / (jnp.sqrt(jnp.sum(blended * blended)) + 1e-07)
    for iteration in range(ITERS):
        gram_matrix = jnp.dot(iterate.T, iterate, precision=lax.Precision.HIGHEST, preferred_element_type=jnp.float32)
        polynomial = coef_b * gram_matrix + coef_c * jnp.dot(gram_matrix, gram_matrix, precision=lax.Precision.HIGHEST, preferred_element_type=jnp.float32)
        iterate = coef_a * iterate + jnp.dot(iterate, polynomial, precision=lax.Precision.HIGHEST, preferred_element_type=jnp.float32)
    return iterate

def reference(grads, momentum, slots):

    def accumulate(running, addend):
        return (running + addend.astype(jnp.float32), None)
    gradient_sum, unused = lax.scan(accumulate, jnp.zeros(grads.shape[1:], jnp.float32), grads)
    held_momentum = momentum[slots]
    fresh_momentum = 0.95 * held_momentum + gradient_sum
    blended = gradient_sum + 0.95 * fresh_momentum
    finals = lax.map(orthogonalize, blended)
    factor = 0.2 * math.sqrt(max(KVR, HD))
    updates = (factor * finals).astype(jnp.bfloat16)
    new_momentum = jnp.zeros_like(momentum).at[slots].set(fresh_momentum)
    return (updates, new_momentum)
```

```python
import functools
import math

import jax
import jax.numpy as jnp
from jax import lax
from jax.experimental import pallas as pl
from jax.experimental.pallas import tpu as pltpu
from jax.sharding import PartitionSpec as P

ITERS = 5
coef_a = 3.4445
coef_b = -4.775
coef_c = 2.0315

MESH = pl.DeviceIdType.MESH
NY, NZ, NMP = 4, 16, 8
F32, BF16 = jnp.float32, jnp.bfloat16


def split(value):
    high = value.astype(BF16)
    return high, (value - high.astype(F32)).astype(BF16)


def dot(left, right):
    return jnp.dot(left, right, preferred_element_type=F32)


def product(left, right):
    return dot(left[0], right[0]) + (dot(left[0], right[1]) + dot(left[1], right[0]))


def kernel(
    inverse, slots, grads, momentum, updates, new_momentum,
    held, y_out, y_in, z_out, z_in, rows, final, ordered,
    load_sem, y_ss, y_rs, z_ss, z_rs, mp_ss, mp_rs, gz_ss, gz_rs, gy_ss, gy_rs, out_sem,
):
    dp, mp = lax.axis_index("dp"), lax.axis_index("mp")
    y, z = dp // NZ, lax.rem(dp, NZ)

    def at(dy, dz):
        return (lax.rem(y + dy + NY, NY) * NZ + lax.rem(z + dz + NZ, NZ), mp)

    def remote(src, dst, ss, rs, device):
        return pltpu.make_async_remote_copy(
            src_ref=src, dst_ref=dst, send_sem=ss, recv_sem=rs, device_id=device, device_id_type=MESH
        )

    load = pltpu.make_async_copy(grads.at[0], held, load_sem)
    load.start()
    barrier = pltpu.get_barrier_semaphore()
    partners = [at(o, 0) for o in range(1, NY)] + [at(0, 1), at(0, -1)]
    partners += [(dp, lax.rem(mp + o, NMP)) for o in range(1, NMP)]
    for partner in partners:
        pl.semaphore_signal(barrier, inc=1, device_id=partner, device_id_type=MESH)
    load.wait()

    def chunk(dy, dz):
        return held[inverse[lax.rem(y + dy, NY) * NZ + lax.rem(z + dz + NZ, NZ)]]

    def y_copy(o, group, first, count):
        return remote(
            y_out.at[o - 1, pl.ds(first, count)], y_in.at[o - 1, pl.ds(first, count)],
            y_ss.at[o - 1, group], y_rs.at[o - 1, group], at(o, 0),
        )

    def y_single(group, first, dz):
        for o in range(1, NY):
            y_out[o - 1, first] = chunk(o, dz)
            y_copy(o, group, first, 1).start()

    def y_pair(j):
        for o in range(1, NY):
            y_out[o - 1, 2 * j - 1] = chunk(o, 8 - j)
            y_out[o - 1, 2 * j] = chunk(o, j - 8)
            y_copy(o, j, 2 * j - 1, 2).start()

    def y_sum(k, dz):
        total = chunk(0, dz).astype(F32)
        for o in range(NY - 1):
            total = total + y_in[o, k].astype(F32)
        return total

    def z_copy(way, t):
        return remote(z_out.at[way, t], z_in.at[way, t], z_ss.at[way, t], z_rs.at[way, t], at(0, 1 - 2 * way))

    pl.semaphore_wait(barrier, len(partners))
    y_single(0, 0, 8)
    y_pair(1)

    y_pair(2)
    for o in range(1, NY):
        y_copy(o, 0, 0, 1).wait_recv()
    z_out[0, 0] = y_sum(0, 8)
    z_copy(0, 0).start()

    def z_step(t, _):
        @pl.when(t < 6)
        def _():
            y_pair(t + 2)

        @pl.when(t == 6)
        def _():
            y_single(8, 15, 0)

        for o in range(1, NY):
            y_copy(o, t, 2 * t - 1, 2).wait_recv()
        right = y_sum(2 * t - 1, 8 - t)
        left = y_sum(2 * t, t - 8)
        z_copy(0, t - 1).wait_recv()
        z_out[0, t] = right + z_in[0, t - 1]
        z_copy(0, t).start()

        @pl.when(t > 1)
        def _():
            z_copy(1, t - 1).wait_recv()
            z_out[1, t] = left + z_in[1, t - 1]

        @pl.when(t == 1)
        def _():
            z_out[1, t] = left

        z_copy(1, t).start()
        return 0

    lax.fori_loop(1, 8, z_step, 0)
    for o in range(1, NY):
        y_copy(o, 8, 15, 1).wait_recv()
    owned = y_sum(15, 0)
    z_copy(0, 7).wait_recv()
    z_copy(1, 7).wait_recv()
    owned = owned + z_in[0, 7] + z_in[1, 7]
    fresh = 0.95 * momentum[...] + owned
    new_momentum[...] = fresh
    rows[mp] = owned + 0.95 * fresh

    def mp_copy(o):
        return remote(rows.at[mp], rows.at[mp], mp_ss.at[o - 1], mp_rs.at[o - 1], (dp, lax.rem(mp + o, NMP)))

    def mp_arrival(o):
        other = lax.rem(mp + NMP - o, NMP)
        return remote(rows.at[other], rows.at[other], mp_ss.at[o - 1], mp_rs.at[o - 1], (dp, lax.rem(mp + o, NMP)))

    for o in range(1, NMP):
        mp_copy(o).start()
    for o in range(1, NMP):
        mp_arrival(o).wait_recv()

    whole = rows[...].reshape(NMP * 64, 256)
    scale = 1.0 / (jnp.sqrt(jnp.sum(whole * whole, keepdims=True)) + 1e-07)
    whole = whole * scale
    iterate = rows[mp] * scale
    gram = product(split(whole.T), split(whole))
    for iteration in range(ITERS):
        pair = split(gram)
        poly = split(coef_b * gram + coef_c * product(pair, pair))
        iterate = coef_a * iterate + product(split(iterate), poly)
        if iteration + 1 < ITERS:
            half = coef_a * gram + product(pair, poly)
            gram = coef_a * half + product(split(half), poly)
    factor = 0.2 * math.sqrt(max(NMP * 64, 256))
    mine = y * NZ + z
    final[mine] = (factor * iterate).astype(BF16)

    def gz_slot(way, t):
        return y * NZ + lax.rem(z + NZ + (2 * way - 1) * t, NZ)

    def gz_copy(way, t):
        slot = gz_slot(way, t)
        return remote(final.at[slot], final.at[slot], gz_ss.at[way, t], gz_rs.at[way, t], at(0, 1 - 2 * way))

    def gz_wait(way, t):
        slot = gz_slot(way, t + 1)
        remote(final.at[slot], final.at[slot], gz_ss.at[way, t], gz_rs.at[way, t], at(0, 1 - 2 * way)).wait_recv()

    def gy_copy(o, slot, dz):
        return remote(final.at[slot], final.at[slot], gy_ss.at[o - 1, dz], gy_rs.at[o - 1, dz], at(o, 0))

    def gy_send(dz):
        for o in range(1, NY):
            gy_copy(o, y * NZ + lax.rem(z + dz, NZ), dz).start()

    gz_copy(0, 0).start()
    gz_copy(1, 0).start()
    gy_send(0)

    def gz_step(t, _):
        gz_wait(0, t)

        @pl.when(t < 7)
        def _():
            gz_copy(0, t + 1).start()

        gy_send(NZ - 1 - t)

        @pl.when(t < 7)
        def _():
            gz_wait(1, t)

            @pl.when(t < 6)
            def _():
                gz_copy(1, t + 1).start()

            gy_send(t + 1)

        return 0

    lax.fori_loop(0, 8, gz_step, 0)

    def gy_wait(dz, _):
        for o in range(1, NY):
            gy_copy(o, lax.rem(y + NY - o, NY) * NZ + lax.rem(z + dz, NZ), dz).wait_recv()
        return 0

    lax.fori_loop(0, NZ, gy_wait, 0)

    part = 16
    stores = []
    for first in range(0, NY * NZ, part):
        def place(i, _):
            ordered[first + i] = final[slots[first + i]]
            return 0

        lax.fori_loop(0, part, place, 0)
        store = pltpu.make_async_copy(
            ordered.at[pl.ds(first, part)], updates.at[pl.ds(first, part)], out_sem.at[first // part]
        )
        store.start()
        stores.append(store)

    for o in range(1, NY):
        y_copy(o, 0, 0, 1).wait_send()
        y_copy(o, 8, 15, 1).wait_send()
    for o in range(1, NMP):
        mp_copy(o).wait_send()

    def sent(t, _):
        for o in range(1, NY):
            y_copy(o, t, 2 * t - 1, 2).wait_send()
        z_copy(0, t).wait_send()
        z_copy(1, t).wait_send()
        gz_copy(0, t).wait_send()
        gz_copy(1, t - 1).wait_send()
        return 0

    lax.fori_loop(1, 8, sent, 0)
    z_copy(0, 0).wait_send()
    gz_copy(0, 0).wait_send()

    def gy_sent(dz, _):
        for o in range(1, NY):
            gy_copy(o, y * NZ + lax.rem(z + dz, NZ), dz).wait_send()
        return 0

    lax.fori_loop(0, NZ, gy_sent, 0)
    for store in stores:
        store.wait()


def shards(grads, momentum, slots):
    count = slots.shape[0]
    inverse = jnp.sum(
        jnp.where(slots[:, None] == jnp.arange(count)[None, :], jnp.arange(count, dtype=jnp.int32)[:, None], 0), axis=0
    )
    vmem = pl.BlockSpec(memory_space=pltpu.VMEM)
    smem = pl.BlockSpec(memory_space=pltpu.SMEM)
    anywhere = pl.BlockSpec(memory_space=pl.ANY)
    dma = pltpu.SemaphoreType.DMA
    updates, new_momentum = pl.pallas_call(
        kernel,
        out_shape=(
            jax.ShapeDtypeStruct((64, 64, 256), BF16),
            jax.ShapeDtypeStruct((64, 256), F32),
        ),
        in_specs=[smem, smem, anywhere, vmem],
        out_specs=(anywhere, vmem),
        scratch_shapes=[
            pltpu.VMEM((64, 64, 256), BF16),
            pltpu.VMEM((3, 16, 64, 256), BF16),
            pltpu.VMEM((3, 16, 64, 256), BF16),
            pltpu.VMEM((2, 8, 64, 256), F32),
            pltpu.VMEM((2, 8, 64, 256), F32),
            pltpu.VMEM((NMP, 64, 256), F32),
            pltpu.VMEM((64, 64, 256), BF16),
            pltpu.VMEM((64, 64, 256), BF16),
            dma, dma((3, 9)), dma((3, 9)), dma((2, 8)), dma((2, 8)), dma((7,)), dma((7,)),
            dma((2, 8)), dma((2, 8)), dma((3, 16)), dma((3, 16)), dma((4,)),
        ],
        compiler_params=pltpu.CompilerParams(
            collective_id=0, has_side_effects=True, vmem_limit_bytes=48 * 2**20
        ),
    )(inverse, slots, grads, momentum[0])
    return updates, new_momentum[None]


def solution(mesh):
    in_specs = (P("dp", None, "mp", None), P("dp", "mp", None), P())
    out_specs = (P(None, "mp", None), P("dp", "mp", None))
    return jax.shard_map(shards, mesh=mesh, in_specs=in_specs, out_specs=out_specs, check_vma=False)
```

```python
import functools
import math

import jax
import jax.numpy as jnp
from jax import lax
from jax.experimental import pallas as pl
from jax.experimental.pallas import tpu as pltpu
from jax.sharding import PartitionSpec as P

ITERS = 5
coef_a = 3.4445
coef_b = -4.775
coef_c = 2.0315

MESH = pl.DeviceIdType.MESH
NY, NZ, NMP = 4, 16, 8
SUM_PARENT = {8: 7, 7: 6, 6: 5, 5: 3, 4: 3, 3: 0, 2: 1, 1: 0}
SUM_ORDER = (8, 7, 6, 4, 5, 2, 3, 1, 0)
SPREAD_PARENT = {8: 7, 7: 5, 6: 5, 5: 3, 4: 3, 3: 0, 2: 1, 1: 0}
SPREAD_ORDER = (
    ("b", 0), ("m", 1), ("m", 3), ("b", 1), ("m", 2), ("b", 3), ("m", 4), ("m", 5), ("b", 2),
    ("b", 4), ("b", 5), ("m", 6), ("m", 7), ("b", 6), ("b", 7), ("m", 8), ("b", 8),
)
AHEAD = 3
HOPS = sorted({d - p for parent in (SUM_PARENT, SPREAD_PARENT) for d, p in parent.items()})
FIRST = 48
F32, BF16 = jnp.float32, jnp.bfloat16


def split(value):
    high = value.astype(BF16)
    return high, (value - high.astype(F32)).astype(BF16)


def dot(left, right):
    return jnp.dot(left, right, preferred_element_type=F32)


def product(left, right):
    return dot(left[0], right[0]) + (dot(left[0], right[1]) + dot(left[1], right[0]))


def kernel(
    table, grads, momentum, updates, new_momentum,
    held, y_out, y_in, z_out, z_in, rows, final, ordered,
    load_sem, y_ss, y_rs, z_ss, z_rs, mp_ss, mp_rs, g_ss, g_rs, gy_ss, gy_rs, out_sem,
):
    dp, mp = lax.axis_index("dp"), lax.axis_index("mp")
    y, z = dp // NZ, lax.rem(dp, NZ)

    def at(dy, dz):
        return (lax.rem(y + dy + NY, NY) * NZ + lax.rem(z + dz + NZ, NZ), mp)

    def remote(src, dst, ss, rs, device):
        return pltpu.make_async_remote_copy(
            src_ref=src, dst_ref=dst, send_sem=ss, recv_sem=rs, device_id=device, device_id_type=MESH
        )

    load = pltpu.make_async_copy(grads.at[0], held, load_sem)
    load.start()
    barrier = pltpu.get_barrier_semaphore()
    partners = [at(o, 0) for o in range(1, NY)] + [at(0, s * k) for k in HOPS for s in (1, -1)]
    partners += [(dp, lax.rem(mp + o, NMP)) for o in range(1, NMP)]
    for partner in partners:
        pl.semaphore_signal(barrier, inc=1, device_id=partner, device_id_type=MESH)

    def ways(d):
        return ((0, 1), (1, -1)) if 0 < d < 8 else ((0, 1),)

    def children(parent, d):
        return [c for c in parent if parent[c] == d]

    position, spots = {}, 0
    for d in SUM_ORDER:
        position[d] = spots
        spots += len(ways(d))

    def chunk(dy, dz):
        return held[table[0, lax.rem(y + dy, NY) * NZ + lax.rem(z + dz + NZ, NZ)]]

    def y_copy(o, d):
        part = pl.ds(position[d], len(ways(d)))
        return remote(y_out.at[o - 1, part], y_in.at[o - 1, part], y_ss.at[o - 1, d], y_rs.at[o - 1, d], at(o, 0))

    def y_send(d):
        for o in range(1, NY):
            for way, sign in ways(d):
                y_out[o - 1, position[d] + way] = chunk(o, sign * d)
            y_copy(o, d).start()

    def z_copy(way, sign, d):
        return remote(
            z_out.at[way, d - 1], z_in.at[way, d - 1], z_ss.at[way, d - 1], z_rs.at[way, d - 1],
            at(0, sign * (d - SUM_PARENT[d])),
        )

    load.wait()
    pl.semaphore_wait(barrier, len(partners))
    for d in SUM_ORDER[:AHEAD]:
        y_send(d)
    for index, d in enumerate(SUM_ORDER):
        if index + AHEAD < len(SUM_ORDER):
            y_send(SUM_ORDER[index + AHEAD])
        for o in range(1, NY):
            y_copy(o, d).wait_recv()
        for way, sign in ways(d):
            total = chunk(0, sign * d).astype(F32)
            for o in range(1, NY):
                total = total + y_in[o - 1, position[d] + way].astype(F32)
            for side, step in ways(d) if d else ways(1):
                if side == way or d == 0:
                    for c in children(SUM_PARENT, d):
                        if c < 8 or side == 0:
                            z_copy(side, step, c).wait_recv()
                            total = total + z_in[side, c - 1]
            if d:
                z_out[way, d - 1] = total
                z_copy(way, sign, d).start()
    fresh = 0.95 * momentum[...] + total
    new_momentum[...] = fresh
    rows[mp] = total + 0.95 * fresh

    def mp_copy(o):
        return remote(rows.at[mp], rows.at[mp], mp_ss.at[o - 1], mp_rs.at[o - 1], (dp, lax.rem(mp + o, NMP)))

    def mp_arrival(o):
        other = lax.rem(mp + NMP - o, NMP)
        return remote(rows.at[other], rows.at[other], mp_ss.at[o - 1], mp_rs.at[o - 1], (dp, lax.rem(mp + o, NMP)))

    for o in range(1, NMP):
        mp_copy(o).start()
    for o in range(1, NMP):
        mp_arrival(o).wait_recv()

    whole = rows[...].reshape(NMP * 64, 256)
    scale = 1.0 / (jnp.sqrt(jnp.sum(whole * whole, keepdims=True)) + 1e-07)
    whole = whole * scale
    iterate = rows[mp] * scale
    gram = product(split(whole.T), split(whole))
    for iteration in range(ITERS):
        pair = split(gram)
        poly = split(coef_b * gram + coef_c * product(pair, pair))
        if iteration + 1 < ITERS:
            both = jnp.concatenate([gram, iterate], axis=0)
            both = coef_a * both + product(split(both), poly)
            half, iterate = both[:256], both[256:]
            gram = coef_a * half + product(split(half), poly)
        else:
            iterate = coef_a * iterate + product(split(iterate), poly)
    factor = 0.2 * math.sqrt(max(NMP * 64, 256))
    final[0, z] = (factor * iterate).astype(BF16)

    first_rows, other_rows = pl.ds(0, FIRST), pl.ds(FIRST, 64 - FIRST)

    def spread(kind, way, sign, d, step):
        source = d if step == 2 else SPREAD_PARENT[d]
        origin = lax.rem(z + NZ - sign * source, NZ)
        part = final.at[0, origin] if kind == "m" else final.at[pl.ds(1, NY - 1), origin, other_rows]
        which = 0 if kind == "m" else 1
        return remote(part, part, g_ss.at[which, way, d - 1], g_rs.at[which, way, d - 1], at(0, sign * (d - SPREAD_PARENT[d])))

    def across(o, sender_z, rows_of, index):
        return remote(
            final.at[0, sender_z, rows_of], final.at[NY - o, sender_z, rows_of],
            gy_ss.at[o - 1, index], gy_rs.at[o - 1, index], at(o, 0),
        )

    def across_arrival(o, sender_z, rows_of, index):
        return remote(
            final.at[0, sender_z, rows_of], final.at[NY - o, sender_z, rows_of],
            gy_ss.at[o - 1, index], gy_rs.at[o - 1, index], at(o, 0),
        )

    def send_on(kind, d):
        for c in sorted(children(SPREAD_PARENT, d), reverse=True):
            for way, sign in ways(d) if d else ways(1):
                if c < 8 or way == 0:
                    spread(kind, way, sign, c, 1).start()

    def send_across(dz, index):
        for o in range(1, NY):
            across(o, lax.rem(z + dz + NZ, NZ), first_rows, index).start()

    for o in range(1, NY):
        across(o, z, other_rows, 16).start()
    send_on("m", 0)
    send_across(0, 0)
    sent = [(0, 0)]
    for kind, d in SPREAD_ORDER:
        if d == 0:
            for o in range(1, NY):
                across_arrival(o, z, other_rows, 16).wait_recv()
            send_on(kind, 0)
            continue
        for way, sign in ways(d):
            spread(kind, way, sign, d, 2).wait_recv()
            for c in children(SPREAD_PARENT, d):
                if c < 8 or way == 0:
                    spread(kind, way, sign, c, 1).start()
            if kind == "m":
                send_across(-sign * d, len(sent))
                sent.append((-sign * d, len(sent)))
    for dz, index in sent:
        for o in range(1, NY):
            across_arrival(o, lax.rem(z + dz + NZ, NZ), first_rows, index).wait_recv()

    part = 16
    stores = []
    for first in range(0, NY * NZ, part):
        def place(i, _):
            slot = table[1, first + i]
            ordered[first + i] = final[lax.rem(slot // NZ + NY - y, NY), lax.rem(slot, NZ)]
            return 0

        lax.fori_loop(0, part, place, 0)
        store = pltpu.make_async_copy(
            ordered.at[pl.ds(first, part)], updates.at[pl.ds(first, part)], out_sem.at[first // part]
        )
        store.start()
        stores.append(store)

    for d in SUM_ORDER:
        for o in range(1, NY):
            y_copy(o, d).wait_send()
        for way, sign in ways(d):
            if d:
                z_copy(way, sign, d).wait_send()
                spread("m", way, sign, d, 1).wait_send()
                spread("b", way, sign, d, 1).wait_send()
    for o in range(1, NMP):
        mp_copy(o).wait_send()
    for dz, index in sent:
        for o in range(1, NY):
            across(o, lax.rem(z + dz + NZ, NZ), first_rows, index).wait_send()
    for o in range(1, NY):
        across(o, z, other_rows, 16).wait_send()
    for store in stores:
        store.wait()


def shards(grads, momentum, slots):
    matrix = lax.broadcasted_iota(jnp.int32, (2, 64, 64), 1)
    column = lax.broadcasted_iota(jnp.int32, (2, 64, 64), 2)
    forward = lax.broadcasted_iota(jnp.int32, (2, 64, 64), 0) == 1
    slot = slots[None, :, None]
    table = jnp.sum(
        jnp.where(forward, jnp.where(matrix == column, slot, 0), jnp.where(slot == column, matrix, 0)), axis=1
    )
    vmem = pl.BlockSpec(memory_space=pltpu.VMEM)
    smem = pl.BlockSpec(memory_space=pltpu.SMEM)
    anywhere = pl.BlockSpec(memory_space=pl.ANY)
    dma = pltpu.SemaphoreType.DMA
    updates, new_momentum = pl.pallas_call(
        kernel,
        out_shape=(
            jax.ShapeDtypeStruct((64, 64, 256), BF16),
            jax.ShapeDtypeStruct((64, 256), F32),
        ),
        in_specs=[smem, anywhere, vmem],
        out_specs=(anywhere, vmem),
        scratch_shapes=[
            pltpu.VMEM((64, 64, 256), BF16),
            pltpu.VMEM((3, 16, 64, 256), BF16),
            pltpu.VMEM((3, 16, 64, 256), BF16),
            pltpu.VMEM((2, 8, 64, 256), F32),
            pltpu.VMEM((2, 8, 64, 256), F32),
            pltpu.VMEM((NMP, 64, 256), F32),
            pltpu.VMEM((NY, NZ, 64, 256), BF16),
            pltpu.VMEM((64, 64, 256), BF16),
            dma, dma((3, 9)), dma((3, 9)), dma((2, 8)), dma((2, 8)), dma((7,)), dma((7,)),
            dma((2, 2, 8)), dma((2, 2, 8)), dma((3, 17)), dma((3, 17)), dma((4,)),
        ],
        compiler_params=pltpu.CompilerParams(
            collective_id=0, has_side_effects=True, vmem_limit_bytes=50 * 2**20
        ),
    )(table, grads, momentum[0])
    return updates, new_momentum[None]


def solution(mesh):
    in_specs = (P("dp", None, "mp", None), P("dp", "mp", None), P())
    out_specs = (P(None, "mp", None), P("dp", "mp", None))
    return jax.shard_map(shards, mesh=mesh, in_specs=in_specs, out_specs=out_specs, check_vma=False)
```

```python
import functools
import math

import jax
import jax.numpy as jnp
from jax import lax
from jax.experimental import pallas as pl
from jax.experimental.pallas import tpu as pltpu
from jax.sharding import PartitionSpec as P

ITERS = 5
coef_a = 3.4445
coef_b = -4.775
coef_c = 2.0315

MESH = pl.DeviceIdType.MESH
NY, NZ, NMP = 4, 16, 8
SUM_PARENT = {8: 7, 7: 6, 6: 5, 5: 3, 4: 3, 3: 0, 2: 1, 1: 0}
SUM_ORDER = (8, 7, 6, 4, 5, 2, 3, 1, 0)
SPREAD_PARENT = {8: 7, 7: 5, 6: 5, 5: 3, 4: 3, 3: 0, 2: 1, 1: 0}
SPREAD_ORDER = (
    ("b", 0), ("m", 1), ("m", 3), ("b", 1), ("m", 2), ("b", 3), ("m", 4), ("m", 5), ("b", 2),
    ("b", 4), ("b", 5), ("m", 6), ("m", 7), ("b", 6), ("b", 7), ("m", 8), ("b", 8),
)
AHEAD = 3
PIECES = 1
HOPS = sorted({d - p for parent in (SUM_PARENT, SPREAD_PARENT) for d, p in parent.items()})
FIRST = 48
F32, BF16 = jnp.float32, jnp.bfloat16


def split(value):
    high = value.astype(BF16)
    return high, (value - high.astype(F32)).astype(BF16)


def dot(left, right):
    return jnp.dot(left, right, preferred_element_type=F32)


def product(left, right):
    return dot(left[0], right[0]) + (dot(left[0], right[1]) + dot(left[1], right[0]))


def kernel(
    table, grads, momentum, updates, new_momentum,
    held, y_out, y_in, z_out, z_in, rows, final,
    load_sem, y_ss, y_rs, z_ss, z_rs, mp_ss, mp_rs, g_ss, g_rs, gy_ss, gy_rs,
):
    dp, mp = lax.axis_index("dp"), lax.axis_index("mp")
    y, z = dp // NZ, lax.rem(dp, NZ)

    def at(dy, dz):
        return (lax.rem(y + dy + NY, NY) * NZ + lax.rem(z + dz + NZ, NZ), mp)

    def remote(src, dst, ss, rs, device):
        return pltpu.make_async_remote_copy(
            src_ref=src, dst_ref=dst, send_sem=ss, recv_sem=rs, device_id=device, device_id_type=MESH
        )

    load = pltpu.make_async_copy(grads.at[0], held, load_sem)
    load.start()
    barrier = pltpu.get_barrier_semaphore()
    partners = [at(o, 0) for o in range(1, NY)] + [at(0, s * k) for k in HOPS for s in (1, -1)]
    partners += [(dp, lax.rem(mp + 2 * o, NMP)) for o in range(1, 4)] + [(dp, mp + 1 - 2 * lax.rem(mp, 2))]
    for partner in partners:
        pl.semaphore_signal(barrier, inc=1, device_id=partner, device_id_type=MESH)

    def ways(d):
        return ((0, 1), (1, -1)) if 0 < d < 8 else ((0, 1),)

    def children(parent, d):
        return [c for c in parent if parent[c] == d]

    position, spots = {}, 0
    for d in SUM_ORDER:
        position[d] = spots
        spots += len(ways(d))

    def chunk(dy, dz):
        return held[table[0, lax.rem(y + dy, NY) * NZ + lax.rem(z + dz + NZ, NZ)]]

    def y_copy(o, d):
        part = pl.ds(position[d], len(ways(d)))
        return remote(y_out.at[o - 1, part], y_in.at[o - 1, part], y_ss.at[o - 1, d], y_rs.at[o - 1, d], at(o, 0))

    def y_send(d):
        for o in range(1, NY):
            for way, sign in ways(d):
                y_out[o - 1, position[d] + way] = chunk(o, sign * d)
            y_copy(o, d).start()

    def z_copy(way, sign, d):
        return remote(
            z_out.at[way, d - 1], z_in.at[way, d - 1], z_ss.at[way, d - 1], z_rs.at[way, d - 1],
            at(0, sign * (d - SUM_PARENT[d])),
        )

    load.wait()
    pl.semaphore_wait(barrier, len(partners))
    for d in SUM_ORDER[:AHEAD]:
        y_send(d)
    for index, d in enumerate(SUM_ORDER):
        if index + AHEAD < len(SUM_ORDER):
            y_send(SUM_ORDER[index + AHEAD])
        for o in range(1, NY):
            y_copy(o, d).wait_recv()
        for way, sign in ways(d):
            total = chunk(0, sign * d).astype(F32)
            for o in range(1, NY):
                total = total + y_in[o - 1, position[d] + way].astype(F32)
            for side, step in ways(d) if d else ways(1):
                if side == way or d == 0:
                    for c in children(SUM_PARENT, d):
                        if c < 8 or side == 0:
                            z_copy(side, step, c).wait_recv()
                            total = total + z_in[side, c - 1]
            if d:
                z_out[way, d - 1] = total
                z_copy(way, sign, d).start()
    fresh = 0.95 * momentum[...] + total
    new_momentum[...] = fresh
    rows[mp] = total + 0.95 * fresh

    x, core = mp // 2, lax.rem(mp, 2)
    sibling = (dp, 2 * x + 1 - core)
    piece = 64 // PIECES

    def row_copy(index, owner, part, device):
        ref = rows.at[owner, pl.ds(part * piece, piece)]
        return remote(ref, ref, mp_ss.at[index, part], mp_rs.at[index, part], device)

    def chip(o):
        return 2 * lax.rem(x + o, 4) + core

    def pair_of(owner):
        return owner + 1 - 2 * lax.rem(owner, 2)

    def to_chip(o, part):
        return row_copy(o - 1, mp, part, (dp, chip(o)))

    def from_chip(o, part):
        return row_copy(o - 1, chip(4 - o), part, sibling)

    def pass_on(o, part):
        return row_copy(o + 3, chip(4 - o), part, sibling)

    def passed(o, part):
        return row_copy(o + 3, pair_of(chip(4 - o)), part, sibling)

    for part in range(PIECES):
        for o in (2, 1, 3):
            to_chip(o, part).start()
        row_copy(3, mp, part, sibling).start()
    for part in range(PIECES):
        for o in (1, 3, 2):
            from_chip(o, part).wait_recv()
            pass_on(o, part).start()
    for part in range(PIECES):
        row_copy(3, pair_of(mp), part, sibling).wait_recv()
        for o in (1, 3, 2):
            passed(o, part).wait_recv()

    whole = rows[...].reshape(NMP * 64, 256)
    scale = 1.0 / (jnp.sqrt(jnp.sum(whole * whole, keepdims=True)) + 1e-07)
    whole = whole * scale
    iterate = rows[mp] * scale
    gram = product(split(whole.T), split(whole))
    for iteration in range(ITERS):
        pair = split(gram)
        poly = split(coef_b * gram + coef_c * product(pair, pair))
        if iteration + 1 < ITERS:
            both = jnp.concatenate([gram, iterate], axis=0)
            both = coef_a * both + product(split(both), poly)
            half, iterate = both[:256], both[256:]
            gram = coef_a * half + product(split(half), poly)
        else:
            iterate = coef_a * iterate + product(split(iterate), poly)
    factor = 0.2 * math.sqrt(max(NMP * 64, 256))
    final[0, z] = (factor * iterate).astype(BF16)

    first_rows, other_rows = pl.ds(0, FIRST), pl.ds(FIRST, 64 - FIRST)

    def spread(kind, way, sign, d, step):
        source = d if step == 2 else SPREAD_PARENT[d]
        origin = lax.rem(z + NZ - sign * source, NZ)
        part = final.at[0, origin] if kind == "m" else final.at[pl.ds(1, NY - 1), origin, other_rows]
        which = 0 if kind == "m" else 1
        return remote(part, part, g_ss.at[which, way, d - 1], g_rs.at[which, way, d - 1], at(0, sign * (d - SPREAD_PARENT[d])))

    def across(o, sender_z, rows_of, index):
        return remote(
            final.at[0, sender_z, rows_of], final.at[NY - o, sender_z, rows_of],
            gy_ss.at[o - 1, index], gy_rs.at[o - 1, index], at(o, 0),
        )

    def across_arrival(o, sender_z, rows_of, index):
        return remote(
            final.at[0, sender_z, rows_of], final.at[NY - o, sender_z, rows_of],
            gy_ss.at[o - 1, index], gy_rs.at[o - 1, index], at(o, 0),
        )

    def send_on(kind, d):
        for c in sorted(children(SPREAD_PARENT, d), reverse=True):
            for way, sign in ways(d) if d else ways(1):
                if c < 8 or way == 0:
                    spread(kind, way, sign, c, 1).start()

    def send_across(dz, index):
        for o in range(1, NY):
            across(o, lax.rem(z + dz + NZ, NZ), first_rows, index).start()

    for o in range(1, NY):
        across(o, z, other_rows, 16).start()
    send_on("m", 0)
    send_across(0, 0)
    sent = [(0, 0)]
    for kind, d in SPREAD_ORDER:
        if d == 0:
            for o in range(1, NY):
                across_arrival(o, z, other_rows, 16).wait_recv()
            send_on(kind, 0)
            continue
        for way, sign in ways(d):
            spread(kind, way, sign, d, 2).wait_recv()
            for c in children(SPREAD_PARENT, d):
                if c < 8 or way == 0:
                    spread(kind, way, sign, c, 1).start()
        if kind == "m":
            for way, sign in ways(d):
                send_across(-sign * d, len(sent))
                sent.append((-sign * d, len(sent)))
    for dz, index in sent:
        for o in range(1, NY):
            across_arrival(o, lax.rem(z + dz + NZ, NZ), first_rows, index).wait_recv()

    def place(i, _):
        slot = table[1, i]
        updates[i] = final[lax.rem(slot // NZ + NY - y, NY), lax.rem(slot, NZ)]
        return 0

    lax.fori_loop(0, NY * NZ, place, 0)

    for d in SUM_ORDER:
        for o in range(1, NY):
            y_copy(o, d).wait_send()
        for way, sign in ways(d):
            if d:
                z_copy(way, sign, d).wait_send()
                spread("m", way, sign, d, 1).wait_send()
                spread("b", way, sign, d, 1).wait_send()
    for part in range(PIECES):
        row_copy(3, mp, part, sibling).wait_send()
        for o in range(1, 4):
            to_chip(o, part).wait_send()
            pass_on(o, part).wait_send()
    for dz, index in sent:
        for o in range(1, NY):
            across(o, lax.rem(z + dz + NZ, NZ), first_rows, index).wait_send()
    for o in range(1, NY):
        across(o, z, other_rows, 16).wait_send()


def shards(grads, momentum, slots):
    matrix = lax.broadcasted_iota(jnp.int32, (2, 64, 64), 1)
    column = lax.broadcasted_iota(jnp.int32, (2, 64, 64), 2)
    forward = lax.broadcasted_iota(jnp.int32, (2, 64, 64), 0) == 1
    slot = slots[None, :, None]
    table = jnp.sum(
        jnp.where(forward, jnp.where(matrix == column, slot, 0), jnp.where(slot == column, matrix, 0)), axis=1
    )
    vmem = pl.BlockSpec(memory_space=pltpu.VMEM)
    smem = pl.BlockSpec(memory_space=pltpu.SMEM)
    anywhere = pl.BlockSpec(memory_space=pl.ANY)
    dma = pltpu.SemaphoreType.DMA
    updates, new_momentum = pl.pallas_call(
        kernel,
        out_shape=(
            jax.ShapeDtypeStruct((64, 64, 256), BF16),
            jax.ShapeDtypeStruct((64, 256), F32),
        ),
        in_specs=[smem, anywhere, vmem],
        out_specs=(vmem, vmem),
        scratch_shapes=[
            pltpu.VMEM((64, 64, 256), BF16),
            pltpu.VMEM((3, 16, 64, 256), BF16),
            pltpu.VMEM((3, 16, 64, 256), BF16),
            pltpu.VMEM((2, 8, 64, 256), F32),
            pltpu.VMEM((2, 8, 64, 256), F32),
            pltpu.VMEM((NMP, 64, 256), F32),
            pltpu.VMEM((NY, NZ, 64, 256), BF16),
            dma, dma((3, 9)), dma((3, 9)), dma((2, 8)), dma((2, 8)), dma((7, PIECES)), dma((7, PIECES)),
            dma((2, 2, 8)), dma((2, 2, 8)), dma((3, 17)), dma((3, 17)),
        ],
        compiler_params=pltpu.CompilerParams(
            collective_id=0, has_side_effects=True, vmem_limit_bytes=50 * 2**20
        ),
    )(table, grads, momentum[0])
    return updates, new_momentum[None]


def solution(mesh):
    in_specs = (P("dp", None, "mp", None), P("dp", "mp", None), P())
    out_specs = (P(None, "mp", None), P("dp", "mp", None))
    return jax.shard_map(shards, mesh=mesh, in_specs=in_specs, out_specs=out_specs, check_vma=False)
```

```python
import functools
import math

import jax
import jax.numpy as jnp
from jax import lax
from jax.experimental import pallas as pl
from jax.experimental.pallas import tpu as pltpu
from jax.sharding import PartitionSpec as P

ITERS = 5
coef_a = 3.4445
coef_b = -4.775
coef_c = 2.0315

MESH = pl.DeviceIdType.MESH
NY, NZ, NMP = 4, 16, 8
SUM_PARENT = {8: 7, 7: 6, 6: 5, 5: 3, 4: 3, 3: 0, 2: 1, 1: 0}
SUM_ORDER = (8, 7, 6, 4, 5, 2, 3, 1, 0)
SPREAD_PARENT = {8: 7, 7: 5, 6: 5, 5: 3, 4: 3, 3: 0, 2: 1, 1: 0}
SPREAD_ORDER = (
    ("b", 0), ("m", 1), ("m", 3), ("b", 1), ("m", 2), ("b", 3), ("m", 4), ("m", 5), ("b", 2),
    ("b", 4), ("b", 5), ("m", 6), ("m", 7), ("b", 6), ("b", 7), ("m", 8), ("b", 8),
)
AHEAD = 3
PIECES = 1
HOPS = sorted({d - p for parent in (SUM_PARENT, SPREAD_PARENT) for d, p in parent.items()})
FIRST = 48
F32, BF16 = jnp.float32, jnp.bfloat16


def split(value):
    high = value.astype(BF16)
    return high, (value - high.astype(F32)).astype(BF16)


def dot(left, right):
    return jnp.dot(left, right, preferred_element_type=F32)


def product(left, right):
    return dot(left[0], right[0]) + (dot(left[0], right[1]) + dot(left[1], right[0]))


def kernel(
    table, grads, momentum, updates, new_momentum,
    held, y_out, y_in, z_out, z_in, rows, final,
    load_sem, y_ss, y_rs, z_ss, z_rs, mp_ss, mp_rs, g_ss, g_rs, gy_ss, gy_rs,
):
    dp, mp = lax.axis_index("dp"), lax.axis_index("mp")
    y, z = dp // NZ, lax.rem(dp, NZ)

    def at(dy, dz):
        return (lax.rem(y + dy + NY, NY) * NZ + lax.rem(z + dz + NZ, NZ), mp)

    def remote(src, dst, ss, rs, device):
        return pltpu.make_async_remote_copy(
            src_ref=src, dst_ref=dst, send_sem=ss, recv_sem=rs, device_id=device, device_id_type=MESH
        )

    load = pltpu.make_async_copy(grads.at[0], held, load_sem)
    load.start()
    barrier = pltpu.get_barrier_semaphore()
    partners = [at(o, 0) for o in range(1, NY)] + [at(0, s * k) for k in HOPS for s in (1, -1)]
    partners += [(dp, lax.rem(mp + 2 * o, NMP)) for o in range(1, 4)] + [(dp, mp + 1 - 2 * lax.rem(mp, 2))]
    for partner in partners:
        pl.semaphore_signal(barrier, inc=1, device_id=partner, device_id_type=MESH)

    def ways(d):
        return ((0, 1), (1, -1)) if 0 < d < 8 else ((0, 1),)

    def children(parent, d):
        return [c for c in parent if parent[c] == d]

    position, spots = {}, 0
    for d in SUM_ORDER:
        position[d] = spots
        spots += len(ways(d))

    def chunk(dy, dz):
        return held[table[0, lax.rem(y + dy, NY) * NZ + lax.rem(z + dz + NZ, NZ)]]

    def y_copy(o, d):
        part = pl.ds(position[d], len(ways(d)))
        return remote(y_out.at[o - 1, part], y_in.at[o - 1, part], y_ss.at[o - 1, d], y_rs.at[o - 1, d], at(o, 0))

    def y_send(d):
        for o in range(1, NY):
            for way, sign in ways(d):
                y_out[o - 1, position[d] + way] = chunk(o, sign * d)
            y_copy(o, d).start()

    def z_copy(way, sign, d):
        return remote(
            z_out.at[way, d - 1], z_in.at[way, d - 1], z_ss.at[way, d - 1], z_rs.at[way, d - 1],
            at(0, sign * (d - SUM_PARENT[d])),
        )

    load.wait()
    pl.semaphore_wait(barrier, len(partners))
    for d in SUM_ORDER[:AHEAD]:
        y_send(d)
    for index, d in enumerate(SUM_ORDER):
        if index + AHEAD < len(SUM_ORDER):
            y_send(SUM_ORDER[index + AHEAD])
        for o in range(1, NY):
            y_copy(o, d).wait_recv()
        for way, sign in ways(d):
            total = chunk(0, sign * d).astype(F32)
            for o in range(1, NY):
                total = total + y_in[o - 1, position[d] + way].astype(F32)
            for side, step in ways(d) if d else ways(1):
                if side == way or d == 0:
                    for c in children(SUM_PARENT, d):
                        if c < 8 or side == 0:
                            z_copy(side, step, c).wait_recv()
                            total = total + z_in[side, c - 1]
            if d:
                z_out[way, d - 1] = total
                z_copy(way, sign, d).start()
    fresh = 0.95 * momentum[...] + total
    new_momentum[...] = fresh
    rows[mp] = total + 0.95 * fresh

    x, core = mp // 2, lax.rem(mp, 2)
    sibling = (dp, 2 * x + 1 - core)
    piece = 64 // PIECES

    def row_copy(index, owner, part, device):
        ref = rows.at[owner, pl.ds(part * piece, piece)]
        return remote(ref, ref, mp_ss.at[index, part], mp_rs.at[index, part], device)

    def chip(o):
        return 2 * lax.rem(x + o, 4) + core

    def pair_of(owner):
        return owner + 1 - 2 * lax.rem(owner, 2)

    def to_chip(o, part):
        return row_copy(o - 1, mp, part, (dp, chip(o)))

    def from_chip(o, part):
        return row_copy(o - 1, chip(4 - o), part, sibling)

    def pass_on(o, part):
        return row_copy(o + 3, chip(4 - o), part, sibling)

    def passed(o, part):
        return row_copy(o + 3, pair_of(chip(4 - o)), part, sibling)

    for part in range(PIECES):
        for o in (2, 1, 3):
            to_chip(o, part).start()
        row_copy(3, mp, part, sibling).start()
    for d in SUM_ORDER:
        for o in range(1, NY):
            y_copy(o, d).wait_send()
        for way, sign in ways(d):
            if d:
                z_copy(way, sign, d).wait_send()
    for part in range(PIECES):
        for o in (1, 3, 2):
            from_chip(o, part).wait_recv()
            pass_on(o, part).start()
    for part in range(PIECES):
        row_copy(3, pair_of(mp), part, sibling).wait_recv()
        for o in (1, 3, 2):
            passed(o, part).wait_recv()

    whole = rows[...].reshape(NMP * 64, 256)
    scale = 1.0 / (jnp.sqrt(jnp.sum(whole * whole, keepdims=True)) + 1e-07)
    whole = whole * scale
    iterate = rows[mp] * scale
    gram = product(split(whole.T), split(whole))
    for iteration in range(ITERS):
        pair = split(gram)
        poly = split(coef_b * gram + coef_c * product(pair, pair))
        if iteration + 1 < ITERS:
            both = jnp.concatenate([gram, iterate], axis=0)
            both = coef_a * both + product(split(both), poly)
            half, iterate = both[:256], both[256:]
            gram = coef_a * half + product(split(half), poly)
        else:
            iterate = coef_a * iterate + product(split(iterate), poly)
    factor = 0.2 * math.sqrt(max(NMP * 64, 256))
    final[0, z] = (factor * iterate).astype(BF16)

    first_rows, other_rows = pl.ds(0, FIRST), pl.ds(FIRST, 64 - FIRST)

    def spread(kind, way, sign, d, step):
        source = d if step == 2 else SPREAD_PARENT[d]
        origin = lax.rem(z + NZ - sign * source, NZ)
        part = final.at[0, origin] if kind == "m" else final.at[pl.ds(1, NY - 1), origin, other_rows]
        which = 0 if kind == "m" else 1
        return remote(part, part, g_ss.at[which, way, d - 1], g_rs.at[which, way, d - 1], at(0, sign * (d - SPREAD_PARENT[d])))

    def across(o, sender_z, rows_of, index):
        return remote(
            final.at[0, sender_z, rows_of], final.at[NY - o, sender_z, rows_of],
            gy_ss.at[o - 1, index], gy_rs.at[o - 1, index], at(o, 0),
        )

    def across_arrival(o, sender_z, rows_of, index):
        return remote(
            final.at[0, sender_z, rows_of], final.at[NY - o, sender_z, rows_of],
            gy_ss.at[o - 1, index], gy_rs.at[o - 1, index], at(o, 0),
        )

    def send_on(kind, d):
        for c in sorted(children(SPREAD_PARENT, d), reverse=True):
            for way, sign in ways(d) if d else ways(1):
                if c < 8 or way == 0:
                    spread(kind, way, sign, c, 1).start()

    def send_across(dz, index):
        for o in range(1, NY):
            across(o, lax.rem(z + dz + NZ, NZ), first_rows, index).start()

    for o in range(1, NY):
        across(o, z, other_rows, 16).start()
    send_on("m", 0)
    send_across(0, 0)
    sent = [(0, 0)]
    for kind, d in SPREAD_ORDER:
        if d == 0:
            for o in range(1, NY):
                across_arrival(o, z, other_rows, 16).wait_recv()
            send_on(kind, 0)
            continue
        for way, sign in ways(d):
            spread(kind, way, sign, d, 2).wait_recv()
            for c in children(SPREAD_PARENT, d):
                if c < 8 or way == 0:
                    spread(kind, way, sign, c, 1).start()
        if kind == "m":
            for way, sign in ways(d):
                send_across(-sign * d, len(sent))
                sent.append((-sign * d, len(sent)))
    for part in range(PIECES):
        row_copy(3, mp, part, sibling).wait_send()
        for o in range(1, 4):
            to_chip(o, part).wait_send()
            pass_on(o, part).wait_send()
    for d in SUM_ORDER:
        for way, sign in ways(d):
            if d:
                spread("m", way, sign, d, 1).wait_send()
                spread("b", way, sign, d, 1).wait_send()
    for dz, index in sent:
        for o in range(1, NY):
            across(o, lax.rem(z + dz + NZ, NZ), first_rows, index).wait_send()
    for o in range(1, NY):
        across(o, z, other_rows, 16).wait_send()
    for dz, index in sent:
        for o in range(1, NY):
            across_arrival(o, lax.rem(z + dz + NZ, NZ), first_rows, index).wait_recv()

    def place(i, _):
        slot = table[1, i]
        updates[i] = final[lax.rem(slot // NZ + NY - y, NY), lax.rem(slot, NZ)]
        return 0

    lax.fori_loop(0, NY * NZ, place, 0)


def shards(grads, momentum, slots):
    matrix = lax.broadcasted_iota(jnp.int32, (2, 64, 64), 1)
    column = lax.broadcasted_iota(jnp.int32, (2, 64, 64), 2)
    forward = lax.broadcasted_iota(jnp.int32, (2, 64, 64), 0) == 1
    slot = slots[None, :, None]
    table = jnp.sum(
        jnp.where(forward, jnp.where(matrix == column, slot, 0), jnp.where(slot == column, matrix, 0)), axis=1
    )
    vmem = pl.BlockSpec(memory_space=pltpu.VMEM)
    smem = pl.BlockSpec(memory_space=pltpu.SMEM)
    anywhere = pl.BlockSpec(memory_space=pl.ANY)
    dma = pltpu.SemaphoreType.DMA
    updates, new_momentum = pl.pallas_call(
        kernel,
        out_shape=(
            jax.ShapeDtypeStruct((64, 64, 256), BF16),
            jax.ShapeDtypeStruct((64, 256), F32),
        ),
        in_specs=[smem, anywhere, vmem],
        out_specs=(vmem, vmem),
        scratch_shapes=[
            pltpu.VMEM((64, 64, 256), BF16),
            pltpu.VMEM((3, 16, 64, 256), BF16),
            pltpu.VMEM((3, 16, 64, 256), BF16),
            pltpu.VMEM((2, 8, 64, 256), F32),
            pltpu.VMEM((2, 8, 64, 256), F32),
            pltpu.VMEM((NMP, 64, 256), F32),
            pltpu.VMEM((NY, NZ, 64, 256), BF16),
            dma, dma((3, 9)), dma((3, 9)), dma((2, 8)), dma((2, 8)), dma((7, PIECES)), dma((7, PIECES)),
            dma((2, 2, 8)), dma((2, 2, 8)), dma((3, 17)), dma((3, 17)),
        ],
        compiler_params=pltpu.CompilerParams(
            collective_id=0, has_side_effects=True, vmem_limit_bytes=50 * 2**20
        ),
    )(table, grads, momentum[0])
    return updates, new_momentum[None]


def solution(mesh):
    in_specs = (P("dp", None, "mp", None), P("dp", "mp", None), P())
    out_specs = (P(None, "mp", None), P("dp", "mp", None))
    return jax.shard_map(shards, mesh=mesh, in_specs=in_specs, out_specs=out_specs, check_vma=False)
```
